32 devices in a mesh: batch: 4 (over z), seq: 2 (over x), head: 4 (over y, core).
Axes of the slice: x: 2, y: 2, z: 4, core: 2. Of those that a mesh axis runs over, the one named last changes fastest.
Arguments:
- queries: bfloat16 [5120, 8192], P(('batch', 'seq', 'head')), parts along dimension 0, may hold values from -6 to 6
- keys: bfloat16 [5120, 8192], P(('batch', 'seq', 'head')), parts along dimension 0, may hold values from -6 to 6
- values: bfloat16 [5120, 8192], P(('batch', 'seq', 'head')), parts along dimension 0, may hold values from -6 to 6
- group_order: int32 [8, 2], P(('batch', 'seq')), parts along dimension 0, may hold values from 0 to 3, as said below
- gain: float32 [8192], P('head'), may hold values from 0.1 to 1.9
Outputs:
- attended: bfloat16 [5120, 8192], P(('batch', 'seq'), 'head'), parts along dimension 0
The draws below stay inside these ranges and needn't reach their ends.
There are 4 independent parts, one for each index of `batch`. The reference program is written for one: setup_inputs(seed, part) draws one part's arguments, and reference() takes and returns one part's arrays. A program takes and returns all parts, laid end to end along the dimension named above; an argument that names none is the same for every part. Nothing has to cross between parts.
Inputs may be any that keep to these rules, and one draw needn't show every extreme that they name: `group_order`: row d holds d and 3 - d, in either order.
All inputs are finite; a program needn't handle non-finite values.
Results may differ from the reference program's by a relative error of at most 0.01.
Values may be sent and summed in bfloat16 or wider, within the bound.
A program may use at most 64 MiB of HBM per device.

```python
import jax
import jax.numpy as jnp
from jax import lax

HEADS = 64
DH = 128
TOK_DEV = 640
PAIRS = 2
LENGTH = 1280
HD = 8192


def draw_group_order(key, part):
    flips = jax.random.randint(key, (PAIRS,), 0, 2)
    rows = jnp.arange(PAIRS, dtype=jnp.int32)
    mirror = 2 * PAIRS - 1 - rows
    first = jnp.where(flips == 1, mirror, rows)
    second = jnp.where(flips == 1, rows, mirror)
    return jnp.stack([first, second], axis=1).astype(jnp.int32)


def levels(stream_key, dims, split, smallest, high):
    def one(axis_at, parts):
        steps = jax.random.uniform(jax.random.fold_in(jax.random.fold_in(stream_key, 6), axis_at), (parts,), jnp.float32, smallest / len(split), high / len(split))
        return jnp.repeat(jnp.exp(steps), dims[axis_at] // parts).reshape((-1,) + (1,) * (len(dims) - axis_at - 1))

    level = one(*split[0])
    for cut in split[1:]:
        level = level * one(*cut)
    return level


def noise(rng, shape, deviation, reach, shards=(), kind=jnp.bfloat16):
    loudness = levels(rng, shape, shards, -0.22, 0.18) if shards else 1.0
    entries = jax.random.normal(rng, shape, jnp.float32) * deviation * loudness
    return jnp.minimum(jnp.maximum(entries, -reach), reach).astype(kind)


def setup_inputs(seed: int = 0, part: int = 0) -> dict:
    seeds = jax.random.split(jax.random.key(seed), 6)
    part_splits = jax.random.split(jax.random.fold_in(seeds[5], part), 6)
    queries = noise(part_splits[0], (LENGTH, HD), 1.0, 6.0, ((0, 8),))
    keys = noise(part_splits[1], (LENGTH, HD), 1.0, 6.0, ((0, 8),))
    values = noise(part_splits[2], (LENGTH, HD), 1.0, 6.0, ((0, 8),))
    group_order = draw_group_order(jax.random.fold_in(jax.random.fold_in(seeds[5], part), 71), part)
    gain = jnp.clip(1.0 + 0.18 * jax.random.normal(seeds[4], (HD,), jnp.float32), 0.1, 1.9)
    return dict(queries=queries, keys=keys, values=values, group_order=group_order, gain=gain)


def reference(queries, keys, values, group_order, gain):
    half = TOK_DEV // 2
    kc = keys.reshape(PAIRS, 2, half, HEADS, DH).astype(jnp.float32)
    vc = values.reshape(PAIRS, 2, half, HEADS, DH).astype(jnp.float32)
    state = jnp.einsum('cjthd,cjthe->cjhde', kc, vc).astype(jnp.bfloat16)
    state = lax.optimization_barrier(state).astype(jnp.float32)
    low_first = (group_order[:, 0] < PAIRS)[:, None, None, None]
    lows = jnp.where(low_first, state[:, 0], state[:, 1])
    highs = jnp.where(low_first, state[:, 1], state[:, 0])
    low_run = jnp.cumsum(lows, axis=0)
    high_run = jnp.cumsum(highs, axis=0)
    low_prefix = low_run - lows
    high_prefix = lax.optimization_barrier(jnp.sum(lows, axis=0)) - lows + (lax.optimization_barrier(jnp.sum(highs, axis=0)) - high_run)
    prefix = jnp.stack([jnp.where(low_first, low_prefix, high_prefix), jnp.where(low_first, high_prefix, low_prefix)], axis=1)
    prefix_b = prefix.astype(jnp.bfloat16).astype(jnp.float32)
    index = jnp.arange(TOK_DEV, dtype=jnp.int32)
    position = group_order[:, index // half] * half + index % half
    qb = queries.reshape(PAIRS, TOK_DEV, HEADS, DH)
    kb = keys.reshape(PAIRS, TOK_DEV, HEADS, DH)
    vb = values.reshape(PAIRS, TOK_DEV, HEADS, DH)
    gains = gain.reshape(HEADS, DH)

    def one_block(items):
        qx, kx, vx, pre, pos = items
        qf = qx.astype(jnp.float32)
        scores = jnp.einsum('thd,shd->hts', qf, kx.astype(jnp.float32))
        allowed = pos[:, None] >= pos[None, :]
        scores = jnp.where(allowed[None], scores, 0.0).astype(jnp.bfloat16)
        intra = jnp.einsum('hts,she->the', scores.astype(jnp.float32), vx.astype(jnp.float32))
        inter = jnp.einsum('jthd,jhde->jthe', qf.reshape(2, half, HEADS, DH), pre)
        raw = intra + inter.reshape(TOK_DEV, HEADS, DH)
        scale = lax.rsqrt(lax.optimization_barrier(jnp.mean(raw * raw, axis=-1, keepdims=True)) + 1e-06)
        return (raw * scale * gains).astype(jnp.bfloat16).reshape(TOK_DEV, HD)
    blocks = lax.map(one_block, (qb, kb, vb, prefix_b, position))
    return blocks.reshape(LENGTH, HD)
```

```python
import jax
import jax.numpy as jnp
from jax import lax
from jax.experimental import pallas as pl
from jax.experimental.pallas import tpu as pltpu
from jax.sharding import PartitionSpec as P

DH = 128
HC = 4
LAG = 2
MESH = pl.DeviceIdType.MESH
F32 = jnp.float32
BF16 = jnp.bfloat16


def kernel(
    q_hbm, k_hbm, v_hbm, order_ref, gain_hbm, o_hbm,
    qb, kb, vb, raw, ob, own, oth, msg, got, gb,
    lsem, dsend, drecv, ysend, yrecv, xsend, xrecv, osend, orecv, olocal, gsem,
):
    rows = q_hbm.shape[0]
    half = 2 * rows
    nc = qb.shape[0]
    nh = nc // 2
    cw = HC * DH
    width = nh * cw
    x = lax.axis_index("seq")
    me = lax.axis_index("head")
    y, c = lax.div(me, 2), lax.rem(me, 2)
    core = {"head": y * 2 + 1 - c}
    across = {"head": (1 - y) * 2 + c}
    other = {"seq": 1 - x}

    def columns(i, core_of):
        late = lax.div(i, nh)
        dest = (1 - y) * (1 - late) + y * late
        start = (dest * 2 + core_of) * width + lax.rem(i, nh) * cw
        return pl.ds(pl.multiple_of(start, 128), cw)

    arrays = ((q_hbm, qb), (k_hbm, kb), (v_hbm, vb))

    def near(a, i):
        src, dst = arrays[a]
        return pltpu.make_async_copy(src.at[:, columns(i, c)], dst.at[i, c], lsem.at[a, i])

    def swap(a, i):
        src, dst = arrays[a]
        return pltpu.make_async_remote_copy(
            src_ref=src.at[:, columns(i, 1 - c)], dst_ref=dst.at[i, c],
            send_sem=dsend.at[a, i], recv_sem=drecv.at[a, i],
            device_id=core, device_id_type=MESH,
        )

    def turned(j):
        return lax.rem(j + nh, nc)

    def state_copy(j):
        return pltpu.make_async_remote_copy(
            src_ref=own.at[turned(j)], dst_ref=oth.at[j],
            send_sem=ysend.at[j], recv_sem=yrecv.at[j],
            device_id=across, device_id_type=MESH,
        )

    def sum_copy(i):
        return pltpu.make_async_remote_copy(
            src_ref=msg.at[i], dst_ref=got.at[i],
            send_sem=xsend.at[i], recv_sem=xrecv.at[i],
            device_id=other, device_id_type=MESH,
        )

    my_rows = pl.ds(pl.multiple_of(y * half, 16), half)

    def out_far(i):
        return pltpu.make_async_remote_copy(
            src_ref=ob.at[i], dst_ref=o_hbm.at[my_rows, pl.ds(pl.multiple_of(i * cw, 128), cw)],
            send_sem=osend.at[i], recv_sem=orecv.at[i],
            device_id=across, device_id_type=MESH,
        )

    def out_near(i):
        return pltpu.make_async_copy(
            ob.at[nh + i], o_hbm.at[my_rows, pl.ds(pl.multiple_of(i * cw, 128), cw)], olocal.at[i]
        )

    gain_far = pltpu.make_async_remote_copy(
        src_ref=gain_hbm, dst_ref=gb.at[0], send_sem=gsem.at[0], recv_sem=gsem.at[1],
        device_id=across, device_id_type=MESH,
    )
    gain_near = pltpu.make_async_copy(gain_hbm, gb.at[1], gsem.at[2])

    barrier = pltpu.get_barrier_semaphore()
    for partner in (core, across, other):
        pl.semaphore_signal(barrier, inc=1, device_id=partner, device_id_type=MESH)

    def begin_near(j, carry):
        near(1, turned(j)).start()
        near(2, turned(j)).start()
        return carry

    lax.fori_loop(0, nc, begin_near, 0)
    gain_near.start()
    pl.semaphore_wait(barrier, 3)

    def begin_far(j, carry):
        swap(1, turned(j)).start()
        swap(2, turned(j)).start()
        return carry

    def begin_queries(i, carry):
        near(0, i).start()
        swap(0, i).start()
        return carry

    lax.fori_loop(0, nc, begin_far, 0)
    lax.fori_loop(0, nc, begin_queries, 0)
    gain_far.start()

    row_at = lax.broadcasted_iota(jnp.int32, (half, half), 0)
    col_at = lax.broadcasted_iota(jnp.int32, (half, half), 1)
    allowed = row_at >= col_at

    def head_of(ref, i, h):
        return ref[i, :, :, h * DH : (h + 1) * DH].reshape(half, DH)

    def states(j, carry):
        i = turned(j)
        for a in (1, 2):
            near(a, i).wait()
            swap(a, i).wait_recv()
        for h in range(HC):
            own[i, h] = lax.dot_general(
                head_of(kb, i, h), head_of(vb, i, h), (((0,), (0,)), ((), ())),
                preferred_element_type=F32,
            ).astype(BF16)
        state_copy(j).start()
        return carry

    lax.fori_loop(0, nc, states, 0)

    mine = jnp.where(y == 0, order_ref[0, 0], order_ref[0, 1])
    high = jnp.where(mine >= 2, 1.0, 0.0).astype(F32)
    first = jnp.where(x == 0, 1.0, 0.0).astype(F32)
    own_part = 1.0 - first * high
    oth_part = 1.0 - first * (1.0 - high)
    got_part = 1.0 - first * (1.0 - high)

    def inner(i):
        near(0, i).wait()
        swap(0, i).wait_recv()
        for h in range(HC):
            scores = lax.dot_general(
                head_of(qb, i, h), head_of(kb, i, h), (((1,), (1,)), ((), ())),
                preferred_element_type=F32,
            )
            scores = jnp.where(allowed, scores, 0.0).astype(BF16)
            raw[i, :, h * DH : (h + 1) * DH] = jnp.dot(
                scores, head_of(vb, i, h), preferred_element_type=F32
            )
        state_copy(i).wait_recv()
        msg[i] = (own_part * own[i].astype(F32) + oth_part * oth[i].astype(F32)).astype(BF16)
        sum_copy(i).start()

    def finish(i):
        sum_copy(i).wait_recv()
        for h in range(HC):
            prefix = high * oth[i, h].astype(F32) + got_part * got[i, h].astype(F32)
            total = raw[i, :, h * DH : (h + 1) * DH] + jnp.dot(
                head_of(qb, i, h), prefix.astype(BF16), preferred_element_type=F32
            )
            scale = lax.rsqrt(jnp.mean(total * total, axis=-1, keepdims=True) + 1e-06)
            gains = gb[lax.div(i, nh), pl.ds(lax.rem(i, nh) * HC + h, 1), :]
            ob[i, :, h * DH : (h + 1) * DH] = (total * scale * gains).astype(BF16)

        @pl.when(i < nh)
        def _():
            out_far(i).start()

        @pl.when(i >= nh)
        def _():
            out_near(i - nh).start()

    def head_step(i, carry):
        inner(i)
        return carry

    def both_step(i, carry):
        inner(i)
        finish(i - LAG)
        return carry

    def tail_step(i, carry):
        finish(i)
        return carry

    lax.fori_loop(0, LAG, head_step, 0)
    gain_near.wait()
    gain_far.wait()
    lax.fori_loop(LAG, nc, both_step, 0)
    lax.fori_loop(nc - LAG, nc, tail_step, 0)

    def drain(i, carry):
        for a in range(3):
            swap(a, i).wait_send()
        state_copy(i).wait_send()
        sum_copy(i).wait_send()
        return carry

    def drain_out(i, carry):
        out_far(i).wait()
        out_near(i).wait()
        return carry

    lax.fori_loop(0, nc, drain, 0)
    lax.fori_loop(0, nh, drain_out, 0)


def fused(queries, keys, values, group_order, gain):
    rows = queries.shape[0]
    half = 2 * rows
    local_heads = gain.shape[0] // DH
    nh = local_heads // HC
    nc = 2 * nh
    dma = pltpu.SemaphoreType.DMA
    anywhere = pl.BlockSpec(memory_space=pl.ANY)
    kept = pltpu.VMEM((nc, 2, rows, HC * DH), BF16)
    square = pltpu.VMEM((nc, HC, DH, DH), BF16)
    return pl.pallas_call(
        kernel,
        out_shape=jax.ShapeDtypeStruct((2 * half, local_heads * DH), BF16),
        in_specs=[anywhere] * 3 + [pl.BlockSpec(memory_space=pltpu.SMEM), anywhere],
        out_specs=anywhere,
        scratch_shapes=[
            kept, kept, kept,
            pltpu.VMEM((nc, half, HC * DH), F32),
            pltpu.VMEM((nc, half, HC * DH), BF16),
            square, square, square, square,
            pltpu.VMEM((2, local_heads, DH), F32),
            dma((3, nc)), dma((3, nc)), dma((3, nc)),
            dma((nc,)), dma((nc,)), dma((nc,)), dma((nc,)),
            dma((nh,)), dma((nh,)), dma((nh,)), dma((3,)),
        ],
        compiler_params=pltpu.CompilerParams(
            collective_id=0, has_side_effects=True, vmem_limit_bytes=48 * 1024 * 1024
        ),
    )(queries, keys, values, group_order, gain.reshape(local_heads, DH))


def local(queries, keys, values, group_order, gain):
    q_all, k_all, v_all = (
        lax.all_to_all(queries, "head", split_axis=1, concat_axis=0, tiled=True),
        lax.all_to_all(keys, "head", split_axis=1, concat_axis=0, tiled=True),
        lax.all_to_all(values, "head", split_axis=1, concat_axis=0, tiled=True),
    )
    rows = q_all.shape[0]
    half = rows // 2
    local_heads = gain.shape[0] // DH
    pairs = lax.axis_size("seq")
    here = lax.axis_index("seq")
    qx = q_all.reshape(rows, local_heads, DH)
    kx = k_all.reshape(rows, local_heads, DH)
    vx = v_all.reshape(rows, local_heads, DH)
    kh = kx.reshape(2, half, local_heads, DH)
    vh = vx.reshape(2, half, local_heads, DH)
    state = jnp.einsum("jthd,jthe->jhde", kh, vh, preferred_element_type=jnp.float32).astype(
        jnp.bfloat16
    )
    state = lax.optimization_barrier(state).astype(jnp.float32)
    order = group_order[0]
    low_first = order[0] < pairs
    lows = jnp.where(low_first, state[0], state[1])
    highs = jnp.where(low_first, state[1], state[0])
    empty = jnp.zeros_like(lows)
    low_sum = empty
    high_sum = empty
    piece_low = lax.all_gather(lows[None].astype(jnp.bfloat16), "seq", axis=0, tiled=True).astype(
        jnp.float32
    )
    piece_high = lax.all_gather(highs[None].astype(jnp.bfloat16), "seq", axis=0, tiled=True).astype(
        jnp.float32
    )
    owners = jnp.arange(piece_low.shape[0], dtype=jnp.int32)
    below = (owners < here).astype(jnp.float32)[:, None, None, None]
    other = (owners != here).astype(jnp.float32)[:, None, None, None]
    above = (owners > here).astype(jnp.float32)[:, None, None, None]
    low_sum = low_sum + jnp.sum(piece_low * below, axis=0)
    high_sum = high_sum + jnp.sum(piece_low * other + piece_high * above, axis=0)
    first_pre = jnp.where(low_first, low_sum, high_sum).astype(jnp.bfloat16)
    second_pre = jnp.where(low_first, high_sum, low_sum).astype(jnp.bfloat16)
    index = jnp.arange(rows, dtype=jnp.int32)
    position = order[index // half] * half + index % half
    scores = jnp.einsum("thd,shd->hts", qx, kx, preferred_element_type=jnp.float32)
    allowed = position[:, None] >= position[None, :]
    scores = jnp.where(allowed[None], scores, 0.0).astype(jnp.bfloat16)
    intra = jnp.einsum("hts,she->the", scores, vx, preferred_element_type=jnp.float32)
    qh = qx.reshape(2, half, local_heads, DH)
    first_term = jnp.einsum("thd,hde->the", qh[0], first_pre, preferred_element_type=jnp.float32)
    second_term = jnp.einsum("thd,hde->the", qh[1], second_pre, preferred_element_type=jnp.float32)
    raw = intra + jnp.concatenate([first_term, second_term], axis=0)
    scale = lax.rsqrt(jnp.mean(raw * raw, axis=-1, keepdims=True) + 1e-06)
    gains = gain.reshape(local_heads, DH)
    return (raw * scale * gains).astype(jnp.bfloat16).reshape(rows, local_heads * DH)


def solution(mesh):
    small = mesh.shape["seq"] == 2 and mesh.shape["head"] == 4
    return jax.shard_map(
        fused if small else local,
        mesh=mesh,
        in_specs=(
            P(("batch", "seq", "head"), None),
            P(("batch", "seq", "head"), None),
            P(("batch", "seq", "head"), None),
            P(("batch", "seq"), None),
            P("head"),
        ),
        out_specs=P(("batch", "seq"), "head"),
        check_vma=False,
    )
```

```python
import jax
import jax.numpy as jnp
from jax import lax
from jax.experimental import pallas as pl
from jax.experimental.pallas import tpu as pltpu
from jax.sharding import PartitionSpec as P

DH = 128
HC = 4
LAG = 2
MESH = pl.DeviceIdType.MESH
F32 = jnp.float32
BF16 = jnp.bfloat16


def kernel(
    q_hbm, k_hbm, v_hbm, order_hbm, gain_hbm, o_hbm,
    qb, kb, vb, raw, ob, own, oth, msg, got, gb, order_ref,
    lsem, dsend, drecv, ysend, yrecv, xsend, xrecv, osend, orecv, olocal, gsem,
):
    rows = q_hbm.shape[0]
    half = 2 * rows
    nc = qb.shape[0]
    nh = nc // 2
    cw = HC * DH
    width = nh * cw
    x = lax.axis_index("seq")
    me = lax.axis_index("head")
    y, c = lax.div(me, 2), lax.rem(me, 2)
    core = {"head": y * 2 + 1 - c}
    across = {"head": (1 - y) * 2 + c}
    other = {"seq": 1 - x}

    def columns(i, core_of):
        late = lax.div(i, nh)
        dest = (1 - y) * (1 - late) + y * late
        start = (dest * 2 + core_of) * width + lax.rem(i, nh) * cw
        return pl.ds(pl.multiple_of(start, 128), cw)

    arrays = ((q_hbm, qb), (k_hbm, kb), (v_hbm, vb))

    def near(a, i):
        src, dst = arrays[a]
        return pltpu.make_async_copy(src.at[:, columns(i, c)], dst.at[i, c], lsem.at[a, i])

    def swap(a, i):
        src, dst = arrays[a]
        return pltpu.make_async_remote_copy(
            src_ref=src.at[:, columns(i, 1 - c)], dst_ref=dst.at[i, c],
            send_sem=dsend.at[a, i], recv_sem=drecv.at[a, i],
            device_id=core, device_id_type=MESH,
        )

    def turned(j):
        return lax.rem(j + nh, nc)

    def state_copy(j):
        return pltpu.make_async_remote_copy(
            src_ref=own.at[turned(j)], dst_ref=oth.at[j],
            send_sem=ysend.at[j], recv_sem=yrecv.at[j],
            device_id=across, device_id_type=MESH,
        )

    def sum_copy(i):
        return pltpu.make_async_remote_copy(
            src_ref=msg.at[i], dst_ref=got.at[i],
            send_sem=xsend.at[i], recv_sem=xrecv.at[i],
            device_id=other, device_id_type=MESH,
        )

    my_rows = pl.ds(pl.multiple_of(y * half, 16), half)

    def out_far(i):
        return pltpu.make_async_remote_copy(
            src_ref=ob.at[i], dst_ref=o_hbm.at[my_rows, pl.ds(pl.multiple_of(i * cw, 128), cw)],
            send_sem=osend.at[i], recv_sem=orecv.at[i],
            device_id=across, device_id_type=MESH,
        )

    def out_near(i):
        return pltpu.make_async_copy(
            ob.at[nh + i], o_hbm.at[my_rows, pl.ds(pl.multiple_of(i * cw, 128), cw)], olocal.at[i]
        )

    gain_far = pltpu.make_async_remote_copy(
        src_ref=gain_hbm, dst_ref=gb.at[0], send_sem=gsem.at[0], recv_sem=gsem.at[1],
        device_id=across, device_id_type=MESH,
    )
    order_near = pltpu.make_async_copy(order_hbm, order_ref, gsem.at[3])
    gain_near = pltpu.make_async_copy(gain_hbm, gb.at[1], gsem.at[2])

    barrier = pltpu.get_barrier_semaphore()
    for partner in (core, across, other):
        pl.semaphore_signal(barrier, inc=1, device_id=partner, device_id_type=MESH)

    def begin_near(j, carry):
        near(1, turned(j)).start()
        near(2, turned(j)).start()
        return carry

    lax.fori_loop(0, nc, begin_near, 0)
    gain_near.start()
    order_near.start()
    pl.semaphore_wait(barrier, 3)

    def begin_far(j, carry):
        swap(1, turned(j)).start()
        swap(2, turned(j)).start()
        return carry

    def begin_queries(i, carry):
        near(0, i).start()
        swap(0, i).start()
        return carry

    lax.fori_loop(0, nc, begin_far, 0)
    lax.fori_loop(0, nc, begin_queries, 0)
    gain_far.start()

    row_at = lax.broadcasted_iota(jnp.int32, (half, half), 0)
    col_at = lax.broadcasted_iota(jnp.int32, (half, half), 1)
    allowed = row_at >= col_at

    def head_of(ref, i, h):
        return ref[i, :, :, h * DH : (h + 1) * DH].reshape(half, DH)

    def states(j, carry):
        i = turned(j)
        for a in (1, 2):
            near(a, i).wait()
            swap(a, i).wait_recv()
        for h in range(HC):
            own[i, h] = lax.dot_general(
                head_of(kb, i, h), head_of(vb, i, h), (((0,), (0,)), ((), ())),
                preferred_element_type=F32,
            ).astype(BF16)
        state_copy(j).start()
        return carry

    lax.fori_loop(0, nc, states, 0)

    order_near.wait()
    mine = jnp.where(y == 0, order_ref[0, 0], order_ref[0, 1])
    high = jnp.where(mine >= 2, 1.0, 0.0).astype(F32)
    first = jnp.where(x == 0, 1.0, 0.0).astype(F32)
    own_part = 1.0 - first * high
    oth_part = 1.0 - first * (1.0 - high)
    got_part = 1.0 - first * (1.0 - high)

    def inner(i):
        near(0, i).wait()
        swap(0, i).wait_recv()
        for h in range(HC):
            scores = lax.dot_general(
                head_of(qb, i, h), head_of(kb, i, h), (((1,), (1,)), ((), ())),
                preferred_element_type=F32,
            )
            scores = jnp.where(allowed, scores, 0.0).astype(BF16)
            raw[i, :, h * DH : (h + 1) * DH] = jnp.dot(
                scores, head_of(vb, i, h), preferred_element_type=F32
            )
        state_copy(i).wait_recv()
        msg[i] = (own_part * own[i].astype(F32) + oth_part * oth[i].astype(F32)).astype(BF16)
        sum_copy(i).start()

    def finish(i):
        sum_copy(i).wait_recv()
        for h in range(HC):
            prefix = high * oth[i, h].astype(F32) + got_part * got[i, h].astype(F32)
            total = raw[i, :, h * DH : (h + 1) * DH] + jnp.dot(
                head_of(qb, i, h), prefix.astype(BF16), preferred_element_type=F32
            )
            scale = lax.rsqrt(jnp.mean(total * total, axis=-1, keepdims=True) + 1e-06)
            gains = gb[lax.div(i, nh), pl.ds(lax.rem(i, nh) * HC + h, 1), :]
            ob[i, :, h * DH : (h + 1) * DH] = (total * scale * gains).astype(BF16)

        @pl.when(i < nh)
        def _():
            out_far(i).start()

        @pl.when(i >= nh)
        def _():
            out_near(i - nh).start()

    def head_step(i, carry):
        inner(i)
        return carry

    def both_step(i, carry):
        inner(i)
        finish(i - LAG)
        return carry

    def tail_step(i, carry):
        finish(i)
        return carry

    lax.fori_loop(0, LAG, head_step, 0)
    gain_near.wait()
    gain_far.wait()
    lax.fori_loop(LAG, nc, both_step, 0)
    lax.fori_loop(nc - LAG, nc, tail_step, 0)

    def drain(i, carry):
        for a in range(3):
            swap(a, i).wait_send()
        state_copy(i).wait_send()
        sum_copy(i).wait_send()
        return carry

    def drain_out(i, carry):
        out_far(i).wait()
        out_near(i).wait()
        return carry

    lax.fori_loop(0, nc, drain, 0)
    lax.fori_loop(0, nh, drain_out, 0)


def fused(queries, keys, values, group_order, gain):
    rows = queries.shape[0]
    half = 2 * rows
    local_heads = gain.shape[0] // DH
    nh = local_heads // HC
    nc = 2 * nh
    dma = pltpu.SemaphoreType.DMA
    anywhere = pl.BlockSpec(memory_space=pl.ANY)
    kept = pltpu.VMEM((nc, 2, rows, HC * DH), BF16)
    square = pltpu.VMEM((nc, HC, DH, DH), BF16)
    operands = (queries, keys, values, group_order, gain.reshape(local_heads, DH))
    stored = [pltpu.with_memory_space_constraint(a, pltpu.HBM) for a in operands]
    return pl.pallas_call(
        kernel,
        out_shape=jax.ShapeDtypeStruct((2 * half, local_heads * DH), BF16),
        in_specs=[anywhere] * 5,
        out_specs=anywhere,
        scratch_shapes=[
            kept, kept, kept,
            pltpu.VMEM((nc, half, HC * DH), F32),
            pltpu.VMEM((nc, half, HC * DH), BF16),
            square, square, square, square,
            pltpu.VMEM((2, local_heads, DH), F32),
            pltpu.SMEM((1, 2), jnp.int32),
            dma((3, nc)), dma((3, nc)), dma((3, nc)),
            dma((nc,)), dma((nc,)), dma((nc,)), dma((nc,)),
            dma((nh,)), dma((nh,)), dma((nh,)), dma((4,)),
        ],
        compiler_params=pltpu.CompilerParams(
            collective_id=0, has_side_effects=True, vmem_limit_bytes=48 * 1024 * 1024
        ),
    )(*stored)


def local(queries, keys, values, group_order, gain):
    q_all, k_all, v_all = (
        lax.all_to_all(queries, "head", split_axis=1, concat_axis=0, tiled=True),
        lax.all_to_all(keys, "head", split_axis=1, concat_axis=0, tiled=True),
        lax.all_to_all(values, "head", split_axis=1, concat_axis=0, tiled=True),
    )
    rows = q_all.shape[0]
    half = rows // 2
    local_heads = gain.shape[0] // DH
    pairs = lax.axis_size("seq")
    here = lax.axis_index("seq")
    qx = q_all.reshape(rows, local_heads, DH)
    kx = k_all.reshape(rows, local_heads, DH)
    vx = v_all.reshape(rows, local_heads, DH)
    kh = kx.reshape(2, half, local_heads, DH)
    vh = vx.reshape(2, half, local_heads, DH)
    state = jnp.einsum("jthd,jthe->jhde", kh, vh, preferred_element_type=jnp.float32).astype(
        jnp.bfloat16
    )
    state = lax.optimization_barrier(state).astype(jnp.float32)
    order = group_order[0]
    low_first = order[0] < pairs
    lows = jnp.where(low_first, state[0], state[1])
    highs = jnp.where(low_first, state[1], state[0])
    empty = jnp.zeros_like(lows)
    low_sum = empty
    high_sum = empty
    piece_low = lax.all_gather(lows[None].astype(jnp.bfloat16), "seq", axis=0, tiled=True).astype(
        jnp.float32
    )
    piece_high = lax.all_gather(highs[None].astype(jnp.bfloat16), "seq", axis=0, tiled=True).astype(
        jnp.float32
    )
    owners = jnp.arange(piece_low.shape[0], dtype=jnp.int32)
    below = (owners < here).astype(jnp.float32)[:, None, None, None]
    other = (owners != here).astype(jnp.float32)[:, None, None, None]
    above = (owners > here).astype(jnp.float32)[:, None, None, None]
    low_sum = low_sum + jnp.sum(piece_low * below, axis=0)
    high_sum = high_sum + jnp.sum(piece_low * other + piece_high * above, axis=0)
    first_pre = jnp.where(low_first, low_sum, high_sum).astype(jnp.bfloat16)
    second_pre = jnp.where(low_first, high_sum, low_sum).astype(jnp.bfloat16)
    index = jnp.arange(rows, dtype=jnp.int32)
    position = order[index // half] * half + index % half
    scores = jnp.einsum("thd,shd->hts", qx, kx, preferred_element_type=jnp.float32)
    allowed = position[:, None] >= position[None, :]
    scores = jnp.where(allowed[None], scores, 0.0).astype(jnp.bfloat16)
    intra = jnp.einsum("hts,she->the", scores, vx, preferred_element_type=jnp.float32)
    qh = qx.reshape(2, half, local_heads, DH)
    first_term = jnp.einsum("thd,hde->the", qh[0], first_pre, preferred_element_type=jnp.float32)
    second_term = jnp.einsum("thd,hde->the", qh[1], second_pre, preferred_element_type=jnp.float32)
    raw = intra + jnp.concatenate([first_term, second_term], axis=0)
    scale = lax.rsqrt(jnp.mean(raw * raw, axis=-1, keepdims=True) + 1e-06)
    gains = gain.reshape(local_heads, DH)
    return (raw * scale * gains).astype(jnp.bfloat16).reshape(rows, local_heads * DH)


def solution(mesh):
    small = mesh.shape["seq"] == 2 and mesh.shape["head"] == 4
    return jax.shard_map(
        fused if small else local,
        mesh=mesh,
        in_specs=(
            P(("batch", "seq", "head"), None),
            P(("batch", "seq", "head"), None),
            P(("batch", "seq", "head"), None),
            P(("batch", "seq"), None),
            P("head"),
        ),
        out_specs=P(("batch", "seq"), "head"),
        check_vma=False,
    )
```
